512 devices in a mesh: grp: 16 (over y_lo, x, core), rng: 32 (over y_hi, z).
Axes of the slice: x: 4, y: 4 (y_hi: 2, y_lo: 2; y = y_hi * 2 + y_lo), z: 16, core: 2. Of those that a mesh axis runs over, the one named last changes fastest.
Arguments:
- embed: bfloat16 [196608, 1024], P(('grp', 'rng')), may hold values from -72 to 72
- centroids: bfloat16 [4096, 1024], P('grp'), may hold values from -6 to 6
- reach: int32 [196608], P(('grp', 'rng')), may hold values from 1 to 128, as said below
Outputs:
- smoothed: bfloat16 [196608, 1024], P(('grp', 'rng'))
- log_total: float32 [196608], P(('grp', 'rng'))
The draws below stay inside these ranges and needn't reach their ends.
Inputs may be any that keep to these rules, and one draw needn't show every extreme that they name: Some row has reach exactly 128.
All inputs are finite; a program needn't handle non-finite values.
Results may differ from the reference program's by a relative error of at most 0.0075.
Values may be sent and summed in bfloat16 or wider, within the bound.
A program may use at most 64 MiB of HBM per device.

```python
import jax
import jax.numpy as jnp
from jax import lax

D = 1024
K = 4096
HALO = 128
ROWS_DEV = 384
GROUP_ROWS = 12288
ROWS = 196608
N_GRP = 16
N_RNG = 32


def centroid_table(key):
    inner = jax.random.fold_in(key, 11)
    return jnp.clip(jax.random.normal(inner, (K, D), jnp.float32), -6.0, 6.0)


def draw_centroids(key, part):
    table = centroid_table(key)
    return table.astype(jnp.bfloat16)


def draw_embed(key, part):
    key = jax.random.fold_in(key, 3)
    values = jnp.clip(jax.random.normal(key, (ROWS, D), jnp.float32), -6.0, 6.0)
    return values.astype(jnp.bfloat16)


def draw_reach(key, part):
    key = jax.random.fold_in(key, 9)
    values = jax.random.randint(key, (ROWS,), 1, HALO + 1, jnp.int32)
    return values.at[0].set(HALO)


def setup_inputs(seed: int = 0) -> dict:
    key_list = jax.random.split(jax.random.key(seed), 4)
    return {
        "embed": draw_embed(jax.random.fold_in(key_list[3], 71), 0),
        "centroids": draw_centroids(jax.random.fold_in(key_list[3], 71), 0),
        "reach": draw_reach(jax.random.fold_in(key_list[3], 71), 0),
    }


logit_gain = 3.0

def assign(rows, centroids):
    score = jnp.dot(rows, centroids.T, preferred_element_type=jnp.float32) * (logit_gain / jnp.sqrt(jnp.float32(D)))
    top = lax.optimization_barrier(jnp.max(score, axis=1))
    expo = jnp.exp(score - top[:, None])
    total = lax.optimization_barrier(jnp.sum(expo, axis=1))
    weight = expo.astype(jnp.bfloat16)
    accum = jnp.dot(weight, centroids, preferred_element_type=jnp.float32)
    return ((accum / total[:, None]).astype(jnp.bfloat16), top + jnp.log(total))

def smooth(local, reach_rows, ext_rows, ext_assigned):
    band = jnp.dot(local, ext_rows.T, preferred_element_type=jnp.float32) / jnp.sqrt(jnp.float32(D))
    rows_here = local.shape[0]
    offset = jnp.arange(ext_rows.shape[0], dtype=jnp.int32)[None, :] - (jnp.arange(rows_here, dtype=jnp.int32)[:, None] + HALO)
    inside = (jnp.abs(offset) <= reach_rows[:, None]) & (offset != 0)
    band = jnp.where(inside, band, jnp.float32(-1e+30))
    peak = lax.optimization_barrier(jnp.max(band, axis=1))
    expo = jnp.where(inside, jnp.exp(band - peak[:, None]), jnp.float32(0.0))
    mix = (expo / lax.optimization_barrier(jnp.sum(expo, axis=1))[:, None]).astype(jnp.bfloat16)
    return jnp.dot(mix, ext_assigned, preferred_element_type=jnp.float32).astype(jnp.bfloat16)

def reference(embed, centroids, reach):
    group_x = embed.reshape(N_GRP, GROUP_ROWS, D)
    group_r = reach.reshape(N_GRP, GROUP_ROWS)

    def per_group(args):
        rows, reaches = args
        assigned, lse = assign(rows, centroids)
        padded_x = jnp.concatenate([rows[GROUP_ROWS - HALO:], rows, rows[:HALO]], axis=0)
        padded_y = jnp.concatenate([assigned[GROUP_ROWS - HALO:], assigned, assigned[:HALO]], axis=0)

        def per_block(index):
            start = (index * ROWS_DEV).astype(jnp.int32)
            local = lax.dynamic_slice_in_dim(rows, start, ROWS_DEV, 0)
            reach_rows = lax.dynamic_slice_in_dim(reaches, start, ROWS_DEV, 0)
            ext_rows = lax.dynamic_slice_in_dim(padded_x, start, ROWS_DEV + 2 * HALO, 0)
            ext_assigned = lax.dynamic_slice_in_dim(padded_y, start, ROWS_DEV + 2 * HALO, 0)
            return smooth(local, reach_rows, ext_rows, ext_assigned)
        blocks = lax.map(per_block, jnp.arange(N_RNG, dtype=jnp.int32))
        return (blocks.reshape(GROUP_ROWS, D), lse)
    smoothed, lse = lax.map(per_group, (group_x, group_r))
    return (smoothed.reshape(ROWS, D), lse.reshape(ROWS))
```

```python
import functools

import jax
import jax.numpy as jnp
from jax import lax
from jax.experimental import pallas as pl
from jax.experimental.pallas import tpu as pltpu
from jax.sharding import PartitionSpec as P

HALO = 128
MESH = pl.DeviceIdType.MESH
LOG2E = 1.4426950408889634
LN2 = 0.6931471805599453

SCHEDULE = (
    {"x+": "D0", "x-": "D1", "ya": "D0", "yb": "D1"},
    {"x+": "D1", "x-": "D0", "ya": "n0", "yb": "n1"},
    {
        "x+": (0, "x+"),
        "x-": (0, "x-"),
        "ya": (0, "x+"),
        "yb": (0, "x-"),
        "z+": (0, "x+"),
        "z-": (0, "x-"),
    },
    {
        "x+": (1, "yb"),
        "x-": (1, "ya"),
        "ya": (1, "x-"),
        "yb": (1, "x+"),
        "z+": (1, "x-"),
        "z-": (1, "x+"),
    },
    {"x+": (2, "ya"), "x-": (2, "yb"), "z+": (2, "ya"), "z-": (2, "yb")},
    {"x+": (3, "x+"), "x-": (3, "x-"), "z+": (2, "x+"), "z-": (2, "x-")},
)
N_SLOT = len(SCHEDULE)


def neighbours():
    g, r = lax.axis_index("grp"), lax.axis_index("rng")
    n_rng = lax.axis_size("rng")
    n_z = n_rng // 2
    core, x, y_lo = lax.rem(g, 2), lax.rem(g // 2, 4), g // 8
    z, y_hi = lax.rem(r, n_z), r // n_z

    def grp(xx, yy, cc):
        return (yy * 4 + xx) * 2 + cc

    across = grp(x, 1 - y_lo, core)
    return {
        "x+": (grp(lax.rem(x + 1, 4), y_lo, core), r),
        "x-": (grp(lax.rem(x + 3, 4), y_lo, core), r),
        "ya": (across, r),
        "yb": (across, (1 - y_hi) * n_z + z),
        "z+": (g, y_hi * n_z + lax.rem(z + 1, n_z)),
        "z-": (g, y_hi * n_z + lax.rem(z + n_z - 1, n_z)),
        "sib": (grp(x, y_lo, 1 - core), r),
        "next": (g, lax.rem(r + 1, n_rng)),
        "prev": (g, lax.rem(r + n_rng - 1, n_rng)),
    }, lax.rem(z, 2)


def kernel(
    embed, cent, reach, out, lse, rows, table, acc, peak, part, mix,
    ici_send, ici_recv, sib_send, sib_recv, halo_send, halo_recv, own_sem,
):
    count, width = embed.shape
    block = cent.shape[0]
    quarter = block // 4
    total_rows = count + 2 * HALO
    gain = 3.0 / (width**0.5)
    to_exp2 = gain * LOG2E
    nbr, parity = neighbours()

    barrier = pltpu.get_barrier_semaphore()
    for device in nbr.values():
        pl.semaphore_signal(barrier, inc=1, device_id=device, device_id_type=MESH)

    load_rows = pltpu.make_async_copy(embed, rows.at[pl.ds(0, count)], own_sem.at[0])
    load_own = pltpu.make_async_copy(cent, table.at[pl.ds(0, block)], own_sem.at[1])
    load_rows.start()
    load_own.start()

    base, pieces = [], []
    at = 2 * block
    for slot in SCHEDULE:
        base.append(at)
        pieces.append(list(slot))
        at += 2 * len(slot) * quarter

    def landing(slot, link):
        return pl.ds(base[slot] + pieces[slot].index(link) * quarter, quarter)

    def source(what):
        if isinstance(what, tuple):
            return table.at[landing(*what)]
        half = parity if what[0] == "D" else 1 - parity
        start = pl.multiple_of(half * (2 * quarter) + int(what[1]) * quarter, quarter)
        return cent.at[pl.ds(start, quarter)]

    def ici(slot, link):
        index = list(SCHEDULE[3]).index(link)
        return pltpu.make_async_remote_copy(
            src_ref=source(SCHEDULE[slot][link]),
            dst_ref=table.at[landing(slot, link)],
            send_sem=ici_send.at[slot, index],
            recv_sem=ici_recv.at[slot, index],
            device_id=nbr[link],
            device_id_type=MESH,
        )

    def share(slot):
        if slot < 0:
            src, dst = cent, table.at[pl.ds(block, block)]
        else:
            size = len(pieces[slot]) * quarter
            src = table.at[pl.ds(base[slot], size)]
            dst = table.at[pl.ds(base[slot] + size, size)]
        return pltpu.make_async_remote_copy(
            src_ref=src,
            dst_ref=dst,
            send_sem=sib_send.at[slot + 1],
            recv_sem=sib_recv.at[slot + 1],
            device_id=nbr["sib"],
            device_id_type=MESH,
        )

    copies = [{link: ici(s, link) for link in pieces[s]} for s in range(N_SLOT)]
    shares = [share(s) for s in range(-1, N_SLOT)]
    halo = [
        pltpu.make_async_remote_copy(
            src_ref=embed.at[pl.ds(count - HALO, HALO)],
            dst_ref=rows.at[pl.ds(count, HALO)],
            send_sem=halo_send.at[0],
            recv_sem=halo_recv.at[0],
            device_id=nbr["next"],
            device_id_type=MESH,
        ),
        pltpu.make_async_remote_copy(
            src_ref=embed.at[pl.ds(0, HALO)],
            dst_ref=rows.at[pl.ds(count + HALO, HALO)],
            send_sem=halo_send.at[1],
            recv_sem=halo_recv.at[1],
            device_id=nbr["prev"],
            device_id_type=MESH,
        ),
    ]

    pl.semaphore_wait(barrier, len(nbr))
    for copy in copies[0].values():
        copy.start()
    for copy in halo:
        copy.start()
    shares[0].start()
    for copy in copies[1].values():
        copy.start()

    def score(r, n, c, k):
        return lax.dot_general(
            rows[pl.ds(r, n), :],
            table[pl.ds(c, k), :],
            (((1,), (1,)), ((), ())),
            preferred_element_type=jnp.float32,
        )

    def absorb(s, r, n, c, k, first):
        top = jnp.broadcast_to(jnp.max(s, axis=1, keepdims=True), (n, 128))
        if not first:
            old = peak[pl.ds(r, n), :]
            top = jnp.maximum(old, top)
            scale = jnp.exp2((old - top) * to_exp2)
        weight = jnp.exp2((s - top[:, :1]) * to_exp2)
        lanes = weight[:, :128]
        for j in range(1, k // 128):
            lanes = lanes + weight[:, j * 128 : (j + 1) * 128]
        peak[pl.ds(r, n), :] = top
        value = jnp.dot(
            weight.astype(jnp.bfloat16),
            table[pl.ds(c, k), :],
            preferred_element_type=jnp.float32,
        )
        if first:
            part[pl.ds(r, n), :] = lanes
            acc[pl.ds(r, n), :] = value
        else:
            part[pl.ds(r, n), :] = part[pl.ds(r, n), :] * scale + lanes
            acc[pl.ds(r, n), :] = acc[pl.ds(r, n), :] * scale[:, :1] + value

    def work(units):
        s = score(*units[0][:4])
        for i, unit in enumerate(units):
            later = score(*units[i + 1][:4]) if i + 1 < len(units) else None
            absorb(s, *unit)
            s = later

    def halves(r, n, c, k, first=False):
        return [(r, n // 2, c, k, first), (r + n // 2, n // 2, c, k, first)]

    load_rows.wait()
    load_own.wait()
    shares[0].wait_recv()
    work(halves(0, count, 0, 2 * block, True))

    for slot in range(N_SLOT):
        for copy in copies[slot].values():
            copy.wait_recv()
        shares[slot + 1].start()
        if slot + 2 < N_SLOT:
            for copy in copies[slot + 2].values():
                copy.start()
        size = 2 * len(pieces[slot]) * quarter
        if slot == 1:
            for copy in halo:
                copy.wait_recv()
            work([(count, 2 * HALO, 0, 2 * block, True), (count, 2 * HALO, base[0], base[1] - base[0], False)])
        if slot == 4:
            band = lax.dot_general(
                rows[pl.ds(0, count), :],
                rows[...],
                (((1,), (1,)), ((), ())),
                preferred_element_type=jnp.float32,
            )
            band = band * (1.0 / width**0.5)
            column = lax.broadcasted_iota(jnp.int32, (count, total_rows), 1)
            place = column - jnp.where(
                column < count, 0, jnp.where(column < count + HALO, count + HALO, HALO)
            )
            offset = place - lax.broadcasted_iota(jnp.int32, (count, total_rows), 0)
            inside = (jnp.abs(offset) <= reach[...]) & (offset != 0)
            band = jnp.where(inside, band, jnp.float32(-1e30))
            highest = jnp.max(band, axis=1, keepdims=True)
            expo = jnp.where(inside, jnp.exp(band - highest), jnp.float32(0.0))
            mix[...] = (expo / jnp.sum(expo, axis=1, keepdims=True)).astype(jnp.bfloat16)
        shares[slot + 1].wait_recv()
        if slot == 0:
            work(halves(0, count, base[slot], size))
        else:
            work(halves(0, total_rows, base[slot], size))

    total = jnp.sum(part[...], axis=1, keepdims=True)
    assigned = (acc[...] / total).astype(jnp.bfloat16)
    lse[...] = peak[pl.ds(0, count), :1] * gain + jnp.log(total[:count])
    out[...] = jnp.dot(mix[...], assigned, preferred_element_type=jnp.float32).astype(
        jnp.bfloat16
    )

    for slot in range(N_SLOT):
        for copy in copies[slot].values():
            copy.wait_send()
    for copy in shares + halo:
        copy.wait_send()


def shards(embed, centroids, reach):
    count, width = embed.shape
    block = centroids.shape[0]
    total = count + 2 * HALO
    table = block * lax.axis_size("grp")
    vmem = pl.BlockSpec(memory_space=pltpu.VMEM)
    hbm = pl.BlockSpec(memory_space=pl.ANY)
    smoothed, log_total = pl.pallas_call(
        kernel,
        out_shape=(
            jax.ShapeDtypeStruct((count, width), jnp.bfloat16),
            jax.ShapeDtypeStruct((count, 1), jnp.float32),
        ),
        in_specs=[hbm, hbm, vmem],
        out_specs=(vmem, vmem),
        scratch_shapes=[
            pltpu.VMEM((total, width), jnp.bfloat16),
            pltpu.VMEM((table, width), jnp.bfloat16),
            pltpu.VMEM((total, width), jnp.float32),
            pltpu.VMEM((total, 128), jnp.float32),
            pltpu.VMEM((total, 128), jnp.float32),
            pltpu.VMEM((count, total), jnp.bfloat16),
            pltpu.SemaphoreType.DMA((N_SLOT, 6)),
            pltpu.SemaphoreType.DMA((N_SLOT, 6)),
            pltpu.SemaphoreType.DMA((N_SLOT + 1,)),
            pltpu.SemaphoreType.DMA((N_SLOT + 1,)),
            pltpu.SemaphoreType.DMA((2,)),
            pltpu.SemaphoreType.DMA((2,)),
            pltpu.SemaphoreType.DMA((2,)),
        ],
        compiler_params=pltpu.CompilerParams(
            collective_id=0, has_side_effects=True, vmem_limit_bytes=48 * 2**20
        ),
        cost_estimate=pl.CostEstimate(
            flops=4 * total * table * width, bytes_accessed=8 * 2**20, transcendentals=total * table
        ),
    )(embed, centroids, reach[:, None])
    return smoothed, log_total[:, 0]


def solution(mesh):
    return jax.shard_map(
        shards,
        mesh=mesh,
        in_specs=(P(("grp", "rng"), None), P("grp", None), P(("grp", "rng"))),
        out_specs=(P(("grp", "rng"), None), P(("grp", "rng"))),
        check_vma=False,
    )
```

```python
import functools

import jax
import jax.numpy as jnp
from jax import lax
from jax.experimental import pallas as pl
from jax.experimental.pallas import tpu as pltpu
from jax.sharding import PartitionSpec as P

HALO = 128
MESH = pl.DeviceIdType.MESH
LOG2E = 1.4426950408889634
LN2 = 0.6931471805599453

SECOND = -1
SENDS = (
    ("p1", "x+", "D0", 0, 1),
    ("m1", "x-", "D1", 0, 1),
    ("a1", "ya", "n0", 0, 2),
    ("b1", "yb", "n1", 0, 2),
    ("p2", "x+", "D1", SECOND, 2),
    ("m2", "x-", "D0", SECOND, 2),
    ("p3", "x+", "p1", 1, 3),
    ("m3", "x-", "m1", 1, 3),
    ("u1", "z+", "p1", 1, 3),
    ("d1", "z-", "m1", 1, 3),
    ("a2", "ya", "p1", 1, 4),
    ("b2", "yb", "m1", 1, 4),
    ("p4", "x+", "b1", 2, 4),
    ("m4", "x-", "a1", 2, 4),
    ("u2", "z+", "m2", 2, 4),
    ("d2", "z-", "p2", 2, 4),
    ("a3", "ya", "m2", 2, 5),
    ("b3", "yb", "p2", 2, 5),
    ("u3", "z+", "p3", 3, 5),
    ("d3", "z-", "m3", 3, 5),
    ("a4", "ya", "D0", 3, 6),
    ("b4", "yb", "D1", 3, 6),
    ("p5", "x+", "p4", 4, 5),
    ("m5", "x-", "m4", 4, 5),
    ("u4", "z+", "a2", 4, 7),
    ("d4", "z-", "b2", 4, 7),
    ("p6", "x+", "a2", 4, 7),
    ("m6", "x-", "b2", 4, 7),
)
GROUPS = (
    (1, ("p1", "m1")),
    (2, ("p2", "m2", "a1", "b1")),
    (3, ("p3", "m3", "u1", "d1")),
    (4, ("p4", "m4", "u2", "d2")),
    (5, ("p5", "m5", "u3", "d3")),
    (5, ("a2", "b2", "a3", "b3")),
    (6, ("a4", "b4")),
    (7, ("p6", "m6", "u4", "d4")),
)


def neighbours():
    g, r = lax.axis_index("grp"), lax.axis_index("rng")
    n_rng = lax.axis_size("rng")
    n_z = n_rng // 2
    core, x, y_lo = lax.rem(g, 2), lax.rem(g // 2, 4), g // 8
    z, y_hi = lax.rem(r, n_z), r // n_z

    def grp(xx, yy, cc):
        return (yy * 4 + xx) * 2 + cc

    across = grp(x, 1 - y_lo, core)
    return {
        "x+": (grp(lax.rem(x + 1, 4), y_lo, core), r),
        "x-": (grp(lax.rem(x + 3, 4), y_lo, core), r),
        "ya": (across, r),
        "yb": (across, (1 - y_hi) * n_z + z),
        "z+": (g, y_hi * n_z + lax.rem(z + 1, n_z)),
        "z-": (g, y_hi * n_z + lax.rem(z + n_z - 1, n_z)),
        "sib": (grp(x, y_lo, 1 - core), r),
        "next": (g, lax.rem(r + 1, n_rng)),
        "prev": (g, lax.rem(r + n_rng - 1, n_rng)),
    }, lax.rem(z, 2)


def kernel(
    embed, cent, reach_in, out, lse, rows, table, acc, peak, part, band, mix, assigned, reach,
    ici_send, ici_recv, sib_send, sib_recv, halo_send, halo_recv, own_sem,
):
    count, width = embed.shape
    block = cent.shape[0]
    quarter = block // 4
    total_rows = count + 2 * HALO
    gain = 3.0 / (width**0.5)
    to_exp2 = gain * LOG2E
    nbr, parity = neighbours()

    barrier = pltpu.get_barrier_semaphore()
    for device in nbr.values():
        pl.semaphore_signal(barrier, inc=1, device_id=device, device_id_type=MESH)

    load_rows = pltpu.make_async_copy(embed, rows.at[pl.ds(0, count)], own_sem.at[0])
    load_own = pltpu.make_async_copy(cent, table.at[pl.ds(0, block)], own_sem.at[1])
    load_reach = pltpu.make_async_copy(reach_in, reach, own_sem.at[2])
    load_rows.start()
    load_reach.start()
    load_own.start()

    place, base, size = {}, [0], [block]
    for _, names in GROUPS:
        base.append(base[-1] + 2 * size[-1])
        size.append(len(names) * quarter)
        for i, name in enumerate(names):
            place[name] = pl.ds(base[-1] + i * quarter, quarter)

    def source(what):
        if what in place:
            return table.at[place[what]]
        half = parity if what[0] == "D" else 1 - parity
        start = pl.multiple_of(half * (2 * quarter) + int(what[1]) * quarter, quarter)
        return cent.at[pl.ds(start, quarter)]

    copies = []
    for i, (name, link, what, _, _) in enumerate(SENDS):
        copies.append(
            pltpu.make_async_remote_copy(
                src_ref=source(what),
                dst_ref=table.at[place[name]],
                send_sem=ici_send.at[i],
                recv_sem=ici_recv.at[i],
                device_id=nbr[link],
                device_id_type=MESH,
            )
        )
    shares = [
        pltpu.make_async_remote_copy(
            src_ref=cent if group == 0 else table.at[pl.ds(base[group], size[group])],
            dst_ref=table.at[pl.ds(base[group] + size[group], size[group])],
            send_sem=sib_send.at[group],
            recv_sem=sib_recv.at[group],
            device_id=nbr["sib"],
            device_id_type=MESH,
        )
        for group in range(len(GROUPS) + 1)
    ]
    halo = [
        pltpu.make_async_remote_copy(
            src_ref=embed.at[pl.ds(start, HALO)],
            dst_ref=rows.at[pl.ds(count + side * HALO, HALO)],
            send_sem=halo_send.at[side],
            recv_sem=halo_recv.at[side],
            device_id=nbr[to],
            device_id_type=MESH,
        )
        for side, (start, to) in enumerate(((count - HALO, "next"), (0, "prev")))
    ]

    def launch(slot):
        for send, copy in zip(SENDS, copies):
            if send[3] == slot:
                copy.start()

    def boundary(slot):
        for send, copy in zip(SENDS, copies):
            if send[4] == slot:
                copy.wait_recv()
        launch(slot)
        for group, (ready, _) in enumerate(((0, ()), *GROUPS)):
            if ready == slot:
                shares[group].start()
        if slot == 0:
            for copy in halo:
                copy.start()

    def score(r, n, c, k):
        return lax.dot_general(
            rows[pl.ds(r, n), :],
            table[pl.ds(c, k), :],
            (((1,), (1,)), ((), ())),
            preferred_element_type=jnp.float32,
        )

    def absorb(s, r, n, c, k, first):
        top = jnp.broadcast_to(jnp.max(s, axis=1, keepdims=True), (n, 128))
        if not first:
            old = peak[pl.ds(r, n), :]
            top = jnp.maximum(old, top)
            scale = jnp.exp2((old - top) * to_exp2)
        weight = jnp.exp2((s - top[:, :1]) * to_exp2)
        lanes = weight[:, :128]
        for j in range(1, k // 128):
            lanes = lanes + weight[:, j * 128 : (j + 1) * 128]
        peak[pl.ds(r, n), :] = top
        value = jnp.dot(
            weight.astype(jnp.bfloat16),
            table[pl.ds(c, k), :],
            preferred_element_type=jnp.float32,
        )
        if first:
            part[pl.ds(r, n), :] = lanes
            acc[pl.ds(r, n), :] = value
        else:
            part[pl.ds(r, n), :] = part[pl.ds(r, n), :] * scale + lanes
            acc[pl.ds(r, n), :] = acc[pl.ds(r, n), :] * scale[:, :1] + value

    def work(units):
        pending = None
        for before, unit in units:
            if before is not None:
                before()
            s = score(*unit[:4])
            if pending is not None:
                absorb(*pending)
            pending = (s, *unit)
        absorb(*pending)

    def inner(a, na, b, nb):
        return lax.dot_general(
            rows[pl.ds(a, na), :],
            rows[pl.ds(b, nb), :],
            (((1,), (1,)), ((), ())),
            preferred_element_type=jnp.float32,
        )

    def other(slot):
        return base[slot] + size[slot]

    pl.semaphore_wait(barrier, len(nbr))
    boundary(0)
    load_rows.wait()
    load_own.wait()
    load_reach.wait()
    local, ghost, every = (0, count), (count, 2 * HALO), (0, total_rows)
    work([(None, (*local, 0, block, True))])
    launch(SECOND)
    band[:, pl.ds(0, count)] = inner(0, count, 0, count)
    for slot in range(1, 4):
        boundary(slot)
        shares[slot - 1].wait_recv()
        work([(None, (*local, other(slot - 1), size[slot - 1] + size[slot], False))])
    boundary(4)
    for copy in halo:
        copy.wait_recv()
    shares[3].wait_recv()
    work(
        [
            (None, (*local, other(3), size[3], False)),
            (None, (*ghost, 0, 4 * block, True)),
            (None, (*ghost, 4 * block, base[4] - 4 * block, False)),
            (shares[4].wait_recv, (*every, base[4], 2 * size[4], False)),
        ]
    )
    band[pl.ds(0, HALO), pl.ds(count, HALO)] = inner(0, HALO, count, HALO)
    band[pl.ds(count - HALO, HALO), pl.ds(count + HALO, HALO)] = inner(
        count - HALO, HALO, count + HALO, HALO
    )
    boundary(5)

    column = lax.broadcasted_iota(jnp.int32, (HALO, total_rows), 1)
    place_of = column - jnp.where(
        column < count, 0, jnp.where(column < count + HALO, count + HALO, HALO)
    )
    row = lax.broadcasted_iota(jnp.int32, (HALO, total_rows), 0)
    for start in range(0, count, HALO):
        width_of = jnp.broadcast_to(reach[pl.ds(start, HALO)][None, :], (HALO, HALO)).T[:, :1]
        offset = place_of - (row + start)
        inside = (jnp.abs(offset) <= width_of) & (offset != 0)
        b = jnp.where(inside, band[pl.ds(start, HALO), :] * (1.0 / width**0.5), jnp.float32(-1e30))
        highest = jnp.max(b, axis=1, keepdims=True)
        expo = jnp.where(inside, jnp.exp(b - highest), jnp.float32(0.0))
        mix[pl.ds(start, HALO), :] = (expo / jnp.sum(expo, axis=1, keepdims=True)).astype(
            jnp.bfloat16
        )

    def shared(group, boundaries=()):
        def wait():
            for slot in boundaries:
                boundary(slot)
            shares[group].wait_recv()

        return wait

    work(
        [
            (shared(5), (*every, base[5], 2 * size[5], False)),
            (shared(6), (*every, base[6], 2 * size[6], False)),
            (shared(7, (6, 7)), (*every, base[7], 2 * size[7], False)),
            (None, (*every, base[8], size[8], False)),
            (shared(8), (*every, other(8), size[8], False)),
        ]
    )

    total = jnp.sum(part[...], axis=1, keepdims=True)
    assigned[...] = (acc[...] * (1.0 / total)).astype(jnp.bfloat16)
    log_total = peak[pl.ds(0, count), :1] * gain + jnp.log(total[:count])
    for start in range(0, count, HALO):
        turned = jnp.broadcast_to(log_total[start : start + HALO], (HALO, HALO)).T
        lse[pl.ds(start, HALO)] = turned[0]
    for r, n, c in ((0, count - HALO, 0), (count - HALO, HALO, HALO)):
        columns = pl.ds(c, count + HALO) if c == 0 else pl.ds(c, total_rows - c)
        out[pl.ds(r, n), :] = jnp.dot(
            mix[pl.ds(r, n), columns], assigned[columns, :], preferred_element_type=jnp.float32
        ).astype(jnp.bfloat16)
    for copy in copies + shares + halo:
        copy.wait_send()


def shards(embed, centroids, reach):
    count, width = embed.shape
    block = centroids.shape[0]
    total = count + 2 * HALO
    table = block * lax.axis_size("grp")
    vmem = pl.BlockSpec(memory_space=pltpu.VMEM)
    hbm = pl.BlockSpec(memory_space=pltpu.HBM)
    smoothed, log_total = pl.pallas_call(
        kernel,
        out_shape=(
            jax.ShapeDtypeStruct((count, width), jnp.bfloat16),
            jax.ShapeDtypeStruct((count,), jnp.float32),
        ),
        in_specs=[hbm, hbm, hbm],
        out_specs=(vmem, vmem),
        scratch_shapes=[
            pltpu.VMEM((total, width), jnp.bfloat16),
            pltpu.VMEM((table, width), jnp.bfloat16),
            pltpu.VMEM((total, width), jnp.float32),
            pltpu.VMEM((total, 128), jnp.float32),
            pltpu.VMEM((total, 128), jnp.float32),
            pltpu.VMEM((count, total), jnp.float32),
            pltpu.VMEM((count, total), jnp.bfloat16),
            pltpu.VMEM((total, width), jnp.bfloat16),
            pltpu.VMEM((count,), jnp.int32),
            pltpu.SemaphoreType.DMA((len(SENDS),)),
            pltpu.SemaphoreType.DMA((len(SENDS),)),
            pltpu.SemaphoreType.DMA((len(GROUPS) + 1,)),
            pltpu.SemaphoreType.DMA((len(GROUPS) + 1,)),
            pltpu.SemaphoreType.DMA((2,)),
            pltpu.SemaphoreType.DMA((2,)),
            pltpu.SemaphoreType.DMA((3,)),
        ],
        compiler_params=pltpu.CompilerParams(
            collective_id=0, has_side_effects=True, vmem_limit_bytes=48 * 2**20
        ),
        cost_estimate=pl.CostEstimate(
            flops=4 * total * table * width, bytes_accessed=8 * 2**20, transcendentals=total * table
        ),
    )(*(pltpu.with_memory_space_constraint(a, pltpu.HBM) for a in (embed, centroids, reach)))
    return smoothed, log_total


def solution(mesh):
    return jax.shard_map(
        shards,
        mesh=mesh,
        in_specs=(P(("grp", "rng"), None), P("grp", None), P(("grp", "rng"))),
        out_specs=(P(("grp", "rng"), None), P(("grp", "rng"))),
        check_vma=False,
    )
```

```python
import functools

import jax
import jax.numpy as jnp
from jax import lax
from jax.experimental import pallas as pl
from jax.experimental.pallas import tpu as pltpu
from jax.sharding import PartitionSpec as P

HALO = 128
MESH = pl.DeviceIdType.MESH
LOG2E = 1.4426950408889634
LN2 = 0.6931471805599453

SECOND = -1
SENDS = (
    ("p1", "x+", "D0", 0, 1),
    ("m1", "x-", "D1", 0, 1),
    ("a1", "ya", "n0", 0, 2),
    ("b1", "yb", "n1", 0, 2),
    ("p2", "x+", "D1", SECOND, 2),
    ("m2", "x-", "D0", SECOND, 2),
    ("p3", "x+", "p1", 1, 3),
    ("m3", "x-", "m1", 1, 3),
    ("u1", "z+", "p1", 1, 3),
    ("d1", "z-", "m1", 1, 3),
    ("a2", "ya", "p1", 1, 4),
    ("b2", "yb", "m1", 1, 4),
    ("p4", "x+", "b1", 2, 4),
    ("m4", "x-", "a1", 2, 4),
    ("u2", "z+", "m2", 2, 4),
    ("d2", "z-", "p2", 2, 4),
    ("a3", "ya", "m2", 2, 5),
    ("b3", "yb", "p2", 2, 5),
    ("u3", "z+", "p3", 3, 5),
    ("d3", "z-", "m3", 3, 5),
    ("a4", "ya", "D0", 3, 6),
    ("b4", "yb", "D1", 3, 6),
    ("p5", "x+", "p4", 4, 5),
    ("m5", "x-", "m4", 4, 5),
    ("u4", "z+", "a2", 4, 7),
    ("d4", "z-", "b2", 4, 7),
    ("p6", "x+", "a2", 4, 7),
    ("m6", "x-", "b2", 4, 7),
)
GROUPS = (
    (1, ("p1", "m1")),
    (2, ("p2", "m2", "a1", "b1")),
    (3, ("p3", "m3", "u1", "d1")),
    (4, ("p4", "m4", "u2", "d2")),
    (5, ("p5", "m5", "u3", "d3")),
    (5, ("a2", "b2", "a3", "b3")),
    (6, ("a4", "b4")),
    (7, ("p6", "m6", "u4", "d4")),
)


def neighbours():
    g, r = lax.axis_index("grp"), lax.axis_index("rng")
    n_rng = lax.axis_size("rng")
    n_z = n_rng // 2
    core, x, y_lo = lax.rem(g, 2), lax.rem(g // 2, 4), g // 8
    z, y_hi = lax.rem(r, n_z), r // n_z

    def grp(xx, yy, cc):
        return (yy * 4 + xx) * 2 + cc

    across = grp(x, 1 - y_lo, core)
    return {
        "x+": (grp(lax.rem(x + 1, 4), y_lo, core), r),
        "x-": (grp(lax.rem(x + 3, 4), y_lo, core), r),
        "ya": (across, r),
        "yb": (across, (1 - y_hi) * n_z + z),
        "z+": (g, y_hi * n_z + lax.rem(z + 1, n_z)),
        "z-": (g, y_hi * n_z + lax.rem(z + n_z - 1, n_z)),
        "sib": (grp(x, y_lo, 1 - core), r),
        "next": (g, lax.rem(r + 1, n_rng)),
        "prev": (g, lax.rem(r + n_rng - 1, n_rng)),
    }, lax.rem(z, 2)


def kernel(
    embed, cent, reach_in, out, lse, rows, table, acc, peak, part, band, mix, assigned, reach,
    ici_send, ici_recv, sib_send, sib_recv, halo_send, halo_recv, own_sem,
):
    count, width = embed.shape
    block = cent.shape[0]
    quarter = block // 4
    total_rows = count + 2 * HALO
    gain = 3.0 / (width**0.5)
    to_exp2 = gain * LOG2E
    nbr, parity = neighbours()

    barrier = pltpu.get_barrier_semaphore()
    for device in nbr.values():
        pl.semaphore_signal(barrier, inc=1, device_id=device, device_id_type=MESH)

    load_rows = pltpu.make_async_copy(embed, rows.at[pl.ds(0, count)], own_sem.at[0])
    load_own = pltpu.make_async_copy(cent, table.at[pl.ds(0, block)], own_sem.at[1])
    load_reach = pltpu.make_async_copy(reach_in, reach, own_sem.at[2])
    load_rows.start()
    load_reach.start()
    load_own.start()

    place, base, size = {}, [0], [block]
    for _, names in GROUPS:
        base.append(base[-1] + 2 * size[-1])
        size.append(len(names) * quarter)
        for i, name in enumerate(names):
            place[name] = pl.ds(base[-1] + i * quarter, quarter)

    def source(what):
        if what in place:
            return table.at[place[what]]
        half = parity if what[0] == "D" else 1 - parity
        start = pl.multiple_of(half * (2 * quarter) + int(what[1]) * quarter, quarter)
        return cent.at[pl.ds(start, quarter)]

    copies = []
    for i, (name, link, what, _, _) in enumerate(SENDS):
        copies.append(
            pltpu.make_async_remote_copy(
                src_ref=source(what),
                dst_ref=table.at[place[name]],
                send_sem=ici_send.at[i],
                recv_sem=ici_recv.at[i],
                device_id=nbr[link],
                device_id_type=MESH,
            )
        )
    shares = [
        pltpu.make_async_remote_copy(
            src_ref=cent if group == 0 else table.at[pl.ds(base[group], size[group])],
            dst_ref=table.at[pl.ds(base[group] + size[group], size[group])],
            send_sem=sib_send.at[group],
            recv_sem=sib_recv.at[group],
            device_id=nbr["sib"],
            device_id_type=MESH,
        )
        for group in range(len(GROUPS) + 1)
    ]
    halo = [
        pltpu.make_async_remote_copy(
            src_ref=embed.at[pl.ds(start, HALO)],
            dst_ref=rows.at[pl.ds(count + side * HALO, HALO)],
            send_sem=halo_send.at[side],
            recv_sem=halo_recv.at[side],
            device_id=nbr[to],
            device_id_type=MESH,
        )
        for side, (start, to) in enumerate(((count - HALO, "next"), (0, "prev")))
    ]

    def launch(slot):
        for send, copy in zip(SENDS, copies):
            if send[3] == slot:
                copy.start()

    def boundary(slot):
        for send, copy in zip(SENDS, copies):
            if send[4] == slot:
                copy.wait_recv()
        launch(slot)
        for group, (ready, _) in enumerate(((0, ()), *GROUPS)):
            if ready == slot:
                shares[group].start()
        if slot == 0:
            for copy in halo:
                copy.start()

    def score(r, n, c, k):
        return lax.dot_general(
            rows[pl.ds(r, n), :],
            table[pl.ds(c, k), :],
            (((1,), (1,)), ((), ())),
            preferred_element_type=jnp.float32,
        )

    def absorb(s, r, n, c, k, first, final=False):
        top = jnp.broadcast_to(jnp.max(s, axis=1, keepdims=True), (n, 128))
        if not first:
            old = peak[pl.ds(r, n), :]
            top = jnp.maximum(old, top)
            scale = jnp.exp2((old - top) * to_exp2)
        weight = jnp.exp2((s - top[:, :1]) * to_exp2)
        lanes = weight[:, :128]
        for j in range(1, k // 128):
            lanes = lanes + weight[:, j * 128 : (j + 1) * 128]
        peak[pl.ds(r, n), :] = top
        value = jnp.dot(
            weight.astype(jnp.bfloat16),
            table[pl.ds(c, k), :],
            preferred_element_type=jnp.float32,
        )
        if final:
            total = jnp.sum(part[pl.ds(r, n), :] * scale + lanes, axis=1, keepdims=True)
            part[pl.ds(r, n), :] = jnp.broadcast_to(total, (n, 128))
            inverse = 1.0 / total
            assigned[pl.ds(r, n), :] = (
                (acc[pl.ds(r, n), :] * scale[:, :1] + value) * inverse
            ).astype(jnp.bfloat16)
        elif first:
            part[pl.ds(r, n), :] = lanes
            acc[pl.ds(r, n), :] = value
        else:
            part[pl.ds(r, n), :] = part[pl.ds(r, n), :] * scale + lanes
            acc[pl.ds(r, n), :] = acc[pl.ds(r, n), :] * scale[:, :1] + value

    def work(units):
        pending = None
        for before, unit in units:
            if before is not None:
                before()
            s = score(*unit[:4])
            if pending is not None:
                absorb(*pending)
            pending = (s, *unit)
        absorb(*pending)

    def inner(a, na, b, nb):
        return lax.dot_general(
            rows[pl.ds(a, na), :],
            rows[pl.ds(b, nb), :],
            (((1,), (1,)), ((), ())),
            preferred_element_type=jnp.float32,
        )

    def other(slot):
        return base[slot] + size[slot]

    pl.semaphore_wait(barrier, len(nbr))
    boundary(0)
    load_rows.wait()
    load_own.wait()
    load_reach.wait()
    local, ghost, every = (0, count), (count, 2 * HALO), (0, total_rows)
    work([(None, (*local, 0, block, True))])
    launch(SECOND)
    band[:, pl.ds(0, count)] = inner(0, count, 0, count)
    for slot in range(1, 4):
        boundary(slot)
        shares[slot - 1].wait_recv()
        work([(None, (*local, other(slot - 1), size[slot - 1] + size[slot], False))])
    boundary(4)
    for copy in halo:
        copy.wait_recv()
    shares[3].wait_recv()
    work(
        [
            (None, (*local, other(3), size[3], False)),
            (None, (*ghost, 0, 4 * block, True)),
            (None, (*ghost, 4 * block, base[4] - 4 * block, False)),
            (shares[4].wait_recv, (*every, base[4], 2 * size[4], False)),
        ]
    )
    band[pl.ds(0, HALO), pl.ds(count, HALO)] = inner(0, HALO, count, HALO)
    band[pl.ds(count - HALO, HALO), pl.ds(count + HALO, HALO)] = inner(
        count - HALO, HALO, count + HALO, HALO
    )
    boundary(5)

    column = lax.broadcasted_iota(jnp.int32, (HALO, total_rows), 1)
    place_of = column - jnp.where(
        column < count, 0, jnp.where(column < count + HALO, count + HALO, HALO)
    )
    row = lax.broadcasted_iota(jnp.int32, (HALO, total_rows), 0)
    for start in range(0, count, HALO):
        width_of = jnp.broadcast_to(reach[pl.ds(start, HALO)][None, :], (HALO, HALO)).T[:, :1]
        offset = place_of - (row + start)
        inside = (jnp.abs(offset) <= width_of) & (offset != 0)
        b = jnp.where(inside, band[pl.ds(start, HALO), :] * (1.0 / width**0.5), jnp.float32(-1e30))
        highest = jnp.max(b, axis=1, keepdims=True)
        expo = jnp.where(inside, jnp.exp(b - highest), jnp.float32(0.0))
        mix[pl.ds(start, HALO), :] = (expo / jnp.sum(expo, axis=1, keepdims=True)).astype(
            jnp.bfloat16
        )

    def shared(group, boundaries=()):
        def wait():
            for slot in boundaries:
                boundary(slot)
            shares[group].wait_recv()

        return wait

    work(
        [
            (shared(5), (*every, base[5], 2 * size[5], False)),
            (shared(6), (*every, base[6], 2 * size[6], False)),
            (shared(7, (6, 7)), (*every, base[7], 2 * size[7] + size[8], False)),
            (shared(8), (*every, other(8), size[8], False, True)),
        ]
    )

    for start in range(0, count, HALO):
        here = pl.ds(start, HALO)
        lse[here] = (peak[here, :] * gain + jnp.log(part[here, :])).T[0]
    for r, n, c in ((0, count - HALO, 0), (count - HALO, HALO, HALO)):
        columns = pl.ds(c, count + HALO) if c == 0 else pl.ds(c, total_rows - c)
        out[pl.ds(r, n), :] = jnp.dot(
            mix[pl.ds(r, n), columns], assigned[columns, :], preferred_element_type=jnp.float32
        ).astype(jnp.bfloat16)
    for copy in copies + shares + halo:
        copy.wait_send()


def shards(embed, centroids, reach):
    count, width = embed.shape
    block = centroids.shape[0]
    total = count + 2 * HALO
    table = block * lax.axis_size("grp")
    vmem = pl.BlockSpec(memory_space=pltpu.VMEM)
    hbm = pl.BlockSpec(memory_space=pltpu.HBM)
    smoothed, log_total = pl.pallas_call(
        kernel,
        out_shape=(
            jax.ShapeDtypeStruct((count, width), jnp.bfloat16),
            jax.ShapeDtypeStruct((count,), jnp.float32),
        ),
        in_specs=[hbm, hbm, hbm],
        out_specs=(vmem, vmem),
        scratch_shapes=[
            pltpu.VMEM((total, width), jnp.bfloat16),
            pltpu.VMEM((table, width), jnp.bfloat16),
            pltpu.VMEM((total, width), jnp.float32),
            pltpu.VMEM((total, 128), jnp.float32),
            pltpu.VMEM((total, 128), jnp.float32),
            pltpu.VMEM((count, total), jnp.float32),
            pltpu.VMEM((count, total), jnp.bfloat16),
            pltpu.VMEM((total, width), jnp.bfloat16),
            pltpu.VMEM((count,), jnp.int32),
            pltpu.SemaphoreType.DMA((len(SENDS),)),
            pltpu.SemaphoreType.DMA((len(SENDS),)),
            pltpu.SemaphoreType.DMA((len(GROUPS) + 1,)),
            pltpu.SemaphoreType.DMA((len(GROUPS) + 1,)),
            pltpu.SemaphoreType.DMA((2,)),
            pltpu.SemaphoreType.DMA((2,)),
            pltpu.SemaphoreType.DMA((3,)),
        ],
        compiler_params=pltpu.CompilerParams(
            collective_id=0, has_side_effects=True, vmem_limit_bytes=48 * 2**20
        ),
        cost_estimate=pl.CostEstimate(
            flops=4 * total * table * width, bytes_accessed=8 * 2**20, transcendentals=total * table
        ),
    )(*(pltpu.with_memory_space_constraint(a, pltpu.HBM) for a in (embed, centroids, reach)))
    return smoothed, log_total


def solution(mesh):
    return jax.shard_map(
        shards,
        mesh=mesh,
        in_specs=(P(("grp", "rng"), None), P("grp", None), P(("grp", "rng"))),
        out_specs=(P(("grp", "rng"), None), P(("grp", "rng"))),
        check_vma=False,
    )
```

```python
import functools

import jax
import jax.numpy as jnp
from jax import lax
from jax.experimental import pallas as pl
from jax.experimental.pallas import tpu as pltpu
from jax.sharding import PartitionSpec as P

HALO = 128
MESH = pl.DeviceIdType.MESH
LOG2E = 1.4426950408889634
LN2 = 0.6931471805599453

SECOND = -1
SENDS = (
    ("p1", "x+", "D0", 0, 1),
    ("m1", "x-", "D1", 0, 1),
    ("a1", "ya", "n0", 0, 2),
    ("b1", "yb", "n1", 0, 2),
    ("p2", "x+", "D1", SECOND, 2),
    ("m2", "x-", "D0", SECOND, 2),
    ("p3", "x+", "p1", 1, 3),
    ("m3", "x-", "m1", 1, 3),
    ("u1", "z+", "p1", 1, 3),
    ("d1", "z-", "m1", 1, 3),
    ("a2", "ya", "p1", 1, 4),
    ("b2", "yb", "m1", 1, 4),
    ("p4", "x+", "b1", 2, 4),
    ("m4", "x-", "a1", 2, 4),
    ("u2", "z+", "m2", 2, 4),
    ("d2", "z-", "p2", 2, 4),
    ("a3", "ya", "m2", 2, 5),
    ("b3", "yb", "p2", 2, 5),
    ("u3", "z+", "p3", 3, 5),
    ("d3", "z-", "m3", 3, 5),
    ("a4", "ya", "D0", 3, 6),
    ("b4", "yb", "D1", 3, 6),
    ("p5", "x+", "p4", 4, 5),
    ("m5", "x-", "m4", 4, 5),
    ("u4", "z+", "a2", 4, 7),
    ("d4", "z-", "b2", 4, 7),
    ("p6", "x+", "a2", 4, 7),
    ("m6", "x-", "b2", 4, 7),
)
GROUPS = (
    (1, ("p1", "m1")),
    (2, ("p2", "m2", "a1", "b1")),
    (3, ("p3", "m3", "u1", "d1")),
    (4, ("p4", "m4", "u2", "d2")),
    (5, ("p5", "m5", "u3", "d3")),
    (5, ("a2", "b2", "a3", "b3")),
    (6, ("a4", "b4")),
    (7, ("p6", "m6", "u4", "d4")),
)


def neighbours():
    g, r = lax.axis_index("grp"), lax.axis_index("rng")
    n_rng = lax.axis_size("rng")
    n_z = n_rng // 2
    core, x, y_lo = lax.rem(g, 2), lax.rem(g // 2, 4), g // 8
    z, y_hi = lax.rem(r, n_z), r // n_z

    def grp(xx, yy, cc):
        return (yy * 4 + xx) * 2 + cc

    across = grp(x, 1 - y_lo, core)
    return {
        "x+": (grp(lax.rem(x + 1, 4), y_lo, core), r),
        "x-": (grp(lax.rem(x + 3, 4), y_lo, core), r),
        "ya": (across, r),
        "yb": (across, (1 - y_hi) * n_z + z),
        "z+": (g, y_hi * n_z + lax.rem(z + 1, n_z)),
        "z-": (g, y_hi * n_z + lax.rem(z + n_z - 1, n_z)),
        "sib": (grp(x, y_lo, 1 - core), r),
        "next": (g, lax.rem(r + 1, n_rng)),
        "prev": (g, lax.rem(r + n_rng - 1, n_rng)),
    }, lax.rem(z, 2)


def kernel(
    embed, cent, reach_in, out, lse, rows, table, acc, peak, part, band, mix, assigned, reach,
    ici_send, ici_recv, sib_send, sib_recv, halo_send, halo_recv, own_sem,
):
    count, width = embed.shape
    block = cent.shape[0]
    quarter = block // 4
    total_rows = count + 2 * HALO
    gain = 3.0 / (width**0.5)
    to_exp2 = gain * LOG2E
    nbr, parity = neighbours()

    barrier = pltpu.get_barrier_semaphore()
    for device in nbr.values():
        pl.semaphore_signal(barrier, inc=1, device_id=device, device_id_type=MESH)

    load_rows = pltpu.make_async_copy(embed, rows.at[pl.ds(0, count)], own_sem.at[0])
    load_own = pltpu.make_async_copy(cent, table.at[pl.ds(0, block)], own_sem.at[1])
    load_reach = pltpu.make_async_copy(reach_in, reach, own_sem.at[2])
    load_rows.start()
    load_reach.start()
    load_own.start()

    place, base, size = {}, [0], [block]
    for _, names in GROUPS:
        base.append(base[-1] + 2 * size[-1])
        size.append(len(names) * quarter)
        for i, name in enumerate(names):
            place[name] = pl.ds(base[-1] + i * quarter, quarter)

    def source(what):
        if what in place:
            return table.at[place[what]]
        half = parity if what[0] == "D" else 1 - parity
        start = pl.multiple_of(half * (2 * quarter) + int(what[1]) * quarter, quarter)
        return cent.at[pl.ds(start, quarter)]

    copies = []
    for i, (name, link, what, _, _) in enumerate(SENDS):
        copies.append(
            pltpu.make_async_remote_copy(
                src_ref=source(what),
                dst_ref=table.at[place[name]],
                send_sem=ici_send.at[i],
                recv_sem=ici_recv.at[i],
                device_id=nbr[link],
                device_id_type=MESH,
            )
        )
    shares = [
        pltpu.make_async_remote_copy(
            src_ref=cent if group == 0 else table.at[pl.ds(base[group], size[group])],
            dst_ref=table.at[pl.ds(base[group] + size[group], size[group])],
            send_sem=sib_send.at[group],
            recv_sem=sib_recv.at[group],
            device_id=nbr["sib"],
            device_id_type=MESH,
        )
        for group in range(len(GROUPS) + 1)
    ]
    halo = [
        pltpu.make_async_remote_copy(
            src_ref=embed.at[pl.ds(start, HALO)],
            dst_ref=rows.at[pl.ds(count + side * HALO, HALO)],
            send_sem=halo_send.at[side],
            recv_sem=halo_recv.at[side],
            device_id=nbr[to],
            device_id_type=MESH,
        )
        for side, (start, to) in enumerate(((count - HALO, "next"), (0, "prev")))
    ]

    def launch(slot):
        for send, copy in zip(SENDS, copies):
            if send[3] == slot:
                copy.start()

    def boundary(slot):
        for send, copy in zip(SENDS, copies):
            if send[4] == slot:
                copy.wait_recv()
        launch(slot)
        for group, (ready, _) in enumerate(((0, ()), *GROUPS)):
            if ready == slot:
                shares[group].start()
        if slot == 0:
            for copy in halo:
                copy.start()

    def score(r, n, c, k):
        return lax.dot_general(
            rows[pl.ds(r, n), :],
            table[pl.ds(c, k), :],
            (((1,), (1,)), ((), ())),
            preferred_element_type=jnp.float32,
        )

    def absorb(s, r, n, c, k, first, final=False):
        top = jnp.broadcast_to(jnp.max(s, axis=1, keepdims=True), (n, 128))
        if not first:
            old = peak[pl.ds(r, n), :]
            top = jnp.maximum(old, top)
            scale = jnp.exp2((old - top) * to_exp2)
        weight = jnp.exp2((s - top[:, :1]) * to_exp2)
        lanes = weight[:, :128]
        for j in range(1, k // 128):
            lanes = lanes + weight[:, j * 128 : (j + 1) * 128]
        peak[pl.ds(r, n), :] = top
        value = jnp.dot(
            weight.astype(jnp.bfloat16),
            table[pl.ds(c, k), :],
            preferred_element_type=jnp.float32,
        )
        if final:
            total = jnp.sum(part[pl.ds(r, n), :] * scale + lanes, axis=1, keepdims=True)
            part[pl.ds(r, n), :] = jnp.broadcast_to(total, (n, 128))
            inverse = 1.0 / total
            assigned[pl.ds(r, n), :] = (
                (acc[pl.ds(r, n), :] * scale[:, :1] + value) * inverse
            ).astype(jnp.bfloat16)
        elif first:
            part[pl.ds(r, n), :] = lanes
            acc[pl.ds(r, n), :] = value
        else:
            part[pl.ds(r, n), :] = part[pl.ds(r, n), :] * scale + lanes
            acc[pl.ds(r, n), :] = acc[pl.ds(r, n), :] * scale[:, :1] + value

    def work(units):
        pending = None
        for before, unit in units:
            if before is not None:
                before()
            s = score(*unit[:4])
            if pending is not None:
                absorb(*pending)
            pending = (s, *unit)
        absorb(*pending)

    def inner(a, na, b, nb):
        return lax.dot_general(
            rows[pl.ds(a, na), :],
            rows[pl.ds(b, nb), :],
            (((1,), (1,)), ((), ())),
            preferred_element_type=jnp.float32,
        )

    def other(slot):
        return base[slot] + size[slot]

    pl.semaphore_wait(barrier, len(nbr))
    boundary(0)
    load_rows.wait()
    load_own.wait()
    load_reach.wait()
    local, ghost, every = (0, count), (count, 2 * HALO), (0, total_rows)
    work([(None, (*local, 0, block, True))])
    launch(SECOND)
    band[:, pl.ds(0, count)] = inner(0, count, 0, count)
    for slot in range(1, 4):
        boundary(slot)
        shares[slot - 1].wait_recv()
        work([(None, (*local, other(slot - 1), size[slot - 1] + size[slot], False))])
    boundary(4)
    for copy in halo:
        copy.wait_recv()
    shares[3].wait_recv()
    work(
        [
            (None, (*local, other(3), size[3], False)),
            (None, (*ghost, 0, 4 * block, True)),
            (None, (*ghost, 4 * block, base[4] - 4 * block, False)),
            (shares[4].wait_recv, (*every, base[4], 2 * size[4], False)),
        ]
    )
    band[pl.ds(0, HALO), pl.ds(count, HALO)] = inner(0, HALO, count, HALO)
    band[pl.ds(count - HALO, HALO), pl.ds(count + HALO, HALO)] = inner(
        count - HALO, HALO, count + HALO, HALO
    )
    boundary(5)

    tile = (HALO, HALO)
    ahead = lax.broadcasted_iota(jnp.int32, tile, 1) - lax.broadcasted_iota(jnp.int32, tile, 0)
    n_tile = count // HALO
    columns_of = {-1: count, n_tile: count + HALO, **{i: i * HALO for i in range(n_tile)}}
    for t in range(n_tile):
        here = pl.ds(t * HALO, HALO)
        reach_of = jnp.broadcast_to(reach[here][None, :], tile).T
        values, masks = [], []
        for step in (-1, 0, 1):
            offset = ahead + step * HALO
            inside = (jnp.abs(offset) <= reach_of) & (offset != 0)
            value = band[here, pl.ds(columns_of[t + step], HALO)] * (1.0 / width**0.5)
            values.append(jnp.where(inside, value, jnp.float32(-1e30)))
            masks.append(inside)
        highest = jnp.max(jnp.maximum(jnp.maximum(*values[:2]), values[2]), axis=1, keepdims=True)
        expo = [
            jnp.where(inside, jnp.exp(value - highest), jnp.float32(0.0))
            for value, inside in zip(values, masks)
        ]
        inverse = 1.0 / jnp.sum(expo[0] + expo[1] + expo[2], axis=1, keepdims=True)
        mix[here, :] = jnp.zeros((HALO, total_rows), jnp.bfloat16)
        for step, e in zip((-1, 0, 1), expo):
            mix[here, pl.ds(columns_of[t + step], HALO)] = (e * inverse).astype(jnp.bfloat16)

    def shared(group, boundaries=()):
        def wait():
            for slot in boundaries:
                boundary(slot)
            shares[group].wait_recv()

        return wait

    work(
        [
            (shared(5), (*every, base[5], 2 * size[5], False)),
            (shared(6), (*every, base[6], 2 * size[6], False)),
            (shared(7, (6, 7)), (*every, base[7], 2 * size[7] + size[8], False)),
            (shared(8), (*every, other(8), size[8], False, True)),
        ]
    )

    for start in range(0, count, HALO):
        here = pl.ds(start, HALO)
        lse[here] = (peak[here, :] * gain + jnp.log(part[here, :])).T[0]
    for r, n, c in ((0, count - HALO, 0), (count - HALO, HALO, HALO)):
        columns = pl.ds(c, count + HALO) if c == 0 else pl.ds(c, total_rows - c)
        out[pl.ds(r, n), :] = jnp.dot(
            mix[pl.ds(r, n), columns], assigned[columns, :], preferred_element_type=jnp.float32
        ).astype(jnp.bfloat16)
    for copy in copies + shares + halo:
        copy.wait_send()


def shards(embed, centroids, reach):
    count, width = embed.shape
    block = centroids.shape[0]
    total = count + 2 * HALO
    table = block * lax.axis_size("grp")
    vmem = pl.BlockSpec(memory_space=pltpu.VMEM)
    hbm = pl.BlockSpec(memory_space=pltpu.HBM)
    smoothed, log_total = pl.pallas_call(
        kernel,
        out_shape=(
            jax.ShapeDtypeStruct((count, width), jnp.bfloat16),
            jax.ShapeDtypeStruct((count,), jnp.float32),
        ),
        in_specs=[hbm, hbm, hbm],
        out_specs=(vmem, vmem),
        scratch_shapes=[
            pltpu.VMEM((total, width), jnp.bfloat16),
            pltpu.VMEM((table, width), jnp.bfloat16),
            pltpu.VMEM((total, width), jnp.float32),
            pltpu.VMEM((total, 128), jnp.float32),
            pltpu.VMEM((total, 128), jnp.float32),
            pltpu.VMEM((count, total), jnp.float32),
            pltpu.VMEM((count, total), jnp.bfloat16),
            pltpu.VMEM((total, width), jnp.bfloat16),
            pltpu.VMEM((count,), jnp.int32),
            pltpu.SemaphoreType.DMA((len(SENDS),)),
            pltpu.SemaphoreType.DMA((len(SENDS),)),
            pltpu.SemaphoreType.DMA((len(GROUPS) + 1,)),
            pltpu.SemaphoreType.DMA((len(GROUPS) + 1,)),
            pltpu.SemaphoreType.DMA((2,)),
            pltpu.SemaphoreType.DMA((2,)),
            pltpu.SemaphoreType.DMA((3,)),
        ],
        compiler_params=pltpu.CompilerParams(
            collective_id=0, has_side_effects=True, vmem_limit_bytes=48 * 2**20
        ),
        cost_estimate=pl.CostEstimate(
            flops=4 * total * table * width, bytes_accessed=8 * 2**20, transcendentals=total * table
        ),
    )(*(pltpu.with_memory_space_constraint(a, pltpu.HBM) for a in (embed, centroids, reach)))
    return smoothed, log_total


def solution(mesh):
    return jax.shard_map(
        shards,
        mesh=mesh,
        in_specs=(P(("grp", "rng"), None), P("grp", None), P(("grp", "rng"))),
        out_specs=(P(("grp", "rng"), None), P(("grp", "rng"))),
        check_vma=False,
    )
```
